32 devices in a mesh: depth: 4 (over y, core), az: 8 (over z, x).
Axes of the slice: x: 2, y: 2, z: 4, core: 2. Of those that a mesh axis runs over, the one named last changes fastest.
Arguments:
- pressure_field: float32 [2, 2048, 4096], P(None, 'depth', 'az'), may hold values from -6 to 6
- block_inverses: float32 [2, 8, 16, 128, 128], P(None, None, 'depth'), may hold values from -1.25 to 1.25, as said below
- lower_spikes: float32 [2, 8, 16, 128], P(None, None, 'depth'), may hold values from -1 to 1, as said below
- upper_spikes: float32 [2, 8, 16, 128], P(None, None, 'depth'), may hold values from -1 to 1, as said below
- pade_weights: float32 [2, 8], replicated, may hold values from -0.08 to 0.08
- layer_wavenumber: float32 [2, 5], replicated, may hold values from -0.4 to 0.4
- layer_index: int32 [16], P('depth'), may hold values from 0 to 4
- depth_coupling: float32 [2048], P('depth'), may hold values from 0.05 to 1
- attenuation: float32 [5, 6], replicated, may hold values from 0.02 to 0.4
- sediment_type: int32 [4096], P('az'), may hold values from 0 to 5
Outputs:
- final_field: float32 [2, 2048, 4096], P(None, 'depth', 'az')
The draws below stay inside these ranges and needn't reach their ends.
Inputs may be any that keep to these rules, and one draw needn't show every extreme that they name: `block_inverses`: complex blocks whose diagonal entries have real parts between 0.75 and 1.25, every other entry smaller in magnitude than the diagonal ones. `lower_spikes`: the last entry of each spike has magnitude below 1. `upper_spikes`: the first entry of each spike has magnitude below 1.
All inputs are finite; a program needn't handle non-finite values.
Results may differ from the reference program's by a relative error of at most 0.0001.
Values sent between devices are 32-bit elements; how exact they have to be, the bound alone decides.
A program may use at most 128 MiB of HBM per device.

```python
import math
from functools import partial
import jax
import jax.numpy as jnp
from jax import lax

BLK = 128
RATIONAL_ORDER = 8
LAYERS = 5
TYPES = 6
STEPS = 2
VERTICAL_GROUPS = 16
DEPTH = 2048
AZ = 4096


def draw_block_inverses(key, part):
    key_a, key_b, key_c, key_d = jax.random.split(jax.random.fold_in(key, 11), 4)
    array_shape = (RATIONAL_ORDER, VERTICAL_GROUPS, BLK, BLK)
    spread = 0.5
    factor = spread * math.sqrt(3.0 / BLK)
    off_re = jax.random.uniform(key_a, array_shape, minval=-1.0, maxval=1.0) * factor
    off_im = jax.random.uniform(key_b, array_shape, minval=-1.0, maxval=1.0) * factor
    diag_re = jax.random.uniform(key_c, (RATIONAL_ORDER, VERTICAL_GROUPS, BLK, 1), minval=0.75, maxval=1.25)
    diag_im = jax.random.uniform(key_d, (RATIONAL_ORDER, VERTICAL_GROUPS, BLK, 1), minval=-0.3, maxval=0.3)
    diagonal_mask = (jnp.arange(BLK)[:, None] == jnp.arange(BLK)[None, :]).astype(jnp.float32)
    real_part = diagonal_mask * diag_re + (1.0 - diagonal_mask) * off_re
    imag_part = diagonal_mask * diag_im + (1.0 - diagonal_mask) * off_im
    return jnp.stack([real_part, imag_part])


def spike_draw(key, tail_point):
    key_a, key_b, key_c, key_d, random_seed_five, key_f, random_seed_seven = jax.random.split(key, 7)
    array_shape = (RATIONAL_ORDER, VERTICAL_GROUPS, BLK)
    body_re = jax.random.uniform(key_a, array_shape, minval=-0.5, maxval=0.5)
    body_im = jax.random.uniform(key_b, array_shape, minval=-0.5, maxval=0.5)
    accessible_groups = jnp.exp(jax.random.uniform(key_c, (RATIONAL_ORDER, 1), minval=0.0, maxval=math.log(2.0 * VERTICAL_GROUPS)))
    noise_scaling = jnp.exp(jax.random.uniform(key_d, (RATIONAL_ORDER, VERTICAL_GROUPS), minval=math.log(0.5), maxval=math.log(2.0)))
    outlier_draw = jax.random.uniform(random_seed_five, (RATIONAL_ORDER, VERTICAL_GROUPS))
    outlier_scaling = jnp.where(outlier_draw < 0.125, jax.random.uniform(random_seed_seven, (RATIONAL_ORDER, VERTICAL_GROUPS), minval=0.5, maxval=0.8), 1.0)
    outlier_height = jnp.exp(-1.0 / (accessible_groups * noise_scaling)) * outlier_scaling
    phase_angle = jax.random.uniform(key_f, (RATIONAL_ORDER, VERTICAL_GROUPS), minval=-math.pi, maxval=math.pi)
    tail_re = outlier_height * jnp.cos(phase_angle)
    tail_im = outlier_height * jnp.sin(phase_angle)
    picked = (jnp.arange(BLK) == tail_point)[None, None, :]
    real_part = jnp.where(picked, tail_re[:, :, None], body_re)
    imag_part = jnp.where(picked, tail_im[:, :, None], body_im)
    return jnp.stack([real_part, imag_part])


def draw_lower_spikes(key, part):
    return spike_draw(jax.random.fold_in(key, 21), BLK - 1)


def draw_upper_spikes(key, part):
    return spike_draw(jax.random.fold_in(key, 22), 0)


def with_ends(drawn, key, smallest, high):
    index_at = [jax.random.randint(jax.random.fold_in(key, axis), (), 0, length) for axis, length in enumerate(drawn.shape)]
    main_axis = drawn.shape.index(max(drawn.shape))
    next_to = index_at[:main_axis] + [(index_at[main_axis] + 1) % drawn.shape[main_axis]] + index_at[main_axis + 1:]
    return drawn.at[tuple(index_at)].set(smallest).at[tuple(next_to)].set(high)


def levels(stream_key, shape, cuts, low, largest):
    factor_of, own = 1.0, jax.random.fold_in(stream_key, 6)
    for position, shards_of in cuts:
        heights = jnp.exp(jax.random.uniform(jax.random.fold_in(own, position), (shards_of,), jnp.float32, low / len(cuts), largest / len(cuts)))
        factor_of = factor_of * jnp.repeat(heights, shape[position] // shards_of).reshape([-1 if axis == position else 1 for axis in range(len(shape))])
    return factor_of


def noise(own_key, extent, width, limit, pieces=(), held_as=jnp.bfloat16):
    result = width * jax.random.normal(own_key, extent, jnp.float32)
    if pieces:
        result = result * levels(own_key, extent, pieces, -0.22, 0.18)
    return jnp.clip(result, -limit, limit).astype(held_as)


def setup_inputs(seed: int = 0) -> dict:
    keys = jax.random.split(jax.random.key(seed), 11)
    return {
        "pressure_field": noise(keys[0], (2, DEPTH, AZ), 1.0, 6.0, ((1, 4), (2, 8)), jnp.float32),
        "block_inverses": draw_block_inverses(jax.random.fold_in(keys[10], 71), 0),
        "lower_spikes": draw_lower_spikes(jax.random.fold_in(keys[10], 71), 0),
        "upper_spikes": draw_upper_spikes(jax.random.fold_in(keys[10], 71), 0),
        "pade_weights": jnp.clip(jax.random.uniform(keys[4], (2, RATIONAL_ORDER), jnp.float32, -0.08, 0.08), -0.08, 0.08),
        "layer_wavenumber": jnp.clip(jax.random.uniform(keys[5], (2, LAYERS), jnp.float32, -0.4, 0.4), -0.4, 0.4),
        "layer_index": with_ends(jax.random.randint(keys[6], (VERTICAL_GROUPS,), 0, LAYERS), jax.random.fold_in(keys[6], 1), 0, LAYERS - 1).astype(jnp.int32),
        "depth_coupling": jnp.clip(jnp.exp(math.log(1.0) - 2.9957323 * jax.random.uniform(keys[7], (DEPTH,), jnp.float32) ** levels(keys[7], (DEPTH,), ((0, 4),), -0.2, 0.2)), 0.05, 1.0),
        "attenuation": jnp.clip(jnp.exp(jax.random.uniform(keys[8], (LAYERS, TYPES), jnp.float32, math.log(0.02), math.log(0.4))), 0.02, 0.4),
        "sediment_type": with_ends(jax.random.randint(keys[9], (AZ,), 0, TYPES), jax.random.fold_in(keys[9], 1), 0, TYPES - 1).astype(jnp.int32),
    }


FULL_PRECISION = lax.Precision.HIGHEST


def solve_term(accum, inputs, shaped_re, shaped_im):
    inverse, lower, upper, weight = inputs
    solved_re = jnp.einsum("bij,bja->bia", inverse[0], shaped_re, precision=FULL_PRECISION) - jnp.einsum("bij,bja->bia", inverse[1], shaped_im, precision=FULL_PRECISION)
    solved_im = jnp.einsum("bij,bja->bia", inverse[0], shaped_im, precision=FULL_PRECISION) + jnp.einsum("bij,bja->bia", inverse[1], shaped_re, precision=FULL_PRECISION)
    zero_row = jnp.zeros(shaped_re.shape[2:], jnp.float32)

    def forward(carried, blocks):
        y_re, y_im, q_re, q_im = blocks
        z_re = y_re - (q_re[:, None] * carried[0] - q_im[:, None] * carried[1])
        z_im = y_im - (q_re[:, None] * carried[1] + q_im[:, None] * carried[0])
        return (z_re[-1], z_im[-1]), (z_re, z_im)

    def backward(carried, blocks):
        z_re, z_im, w_re, w_im = blocks
        x_re = z_re - (w_re[:, None] * carried[0] - w_im[:, None] * carried[1])
        x_im = z_im - (w_re[:, None] * carried[1] + w_im[:, None] * carried[0])
        return (x_re[0], x_im[0]), (x_re, x_im)

    unused, swept = lax.scan(forward, (zero_row, zero_row), (solved_re, solved_im, lower[0], lower[1]))
    unused, final = lax.scan(backward, (zero_row, zero_row), (swept[0], swept[1], upper[0], upper[1]), reverse=True)
    acc_re = accum[0] + weight[0] * final[0] - weight[1] * final[1]
    acc_im = accum[1] + weight[0] * final[1] + weight[1] * final[0]
    return (acc_re, acc_im), None


def reference(pressure_field, block_inverses, lower_spikes, upper_spikes, pade_weights, layer_wavenumber, layer_index, depth_coupling, attenuation, sediment_type):
    wave_rows = jnp.repeat(layer_wavenumber[:, layer_index], BLK, axis=1)
    damping = jnp.repeat(jnp.exp(-attenuation[layer_index][:, sediment_type]), BLK, axis=0)
    wavenum = jnp.arange(AZ, dtype=jnp.int32)
    signed = jnp.where(wavenum < AZ // 2, wavenum, wavenum - AZ).astype(jnp.float32)
    spatial = (2.0 * jnp.pi * signed / AZ) ** 2
    rotation = depth_coupling[:, None] * spatial[None, :]
    turn = lax.complex(jnp.cos(rotation), -jnp.sin(rotation))
    term_inputs = (jnp.moveaxis(block_inverses, 1, 0), jnp.moveaxis(lower_spikes, 1, 0), jnp.moveaxis(upper_spikes, 1, 0), pade_weights.T)
    pressure = pressure_field
    for range_step in range(STEPS):
        padded = jnp.pad(pressure, ((0, 0), (1, 1), (0, 0)))
        laplace = padded[:, 2:] + padded[:, :-2] - 2.0 * pressure
        oper_re = laplace[0] + wave_rows[0][:, None] * pressure[0] - wave_rows[1][:, None] * pressure[1]
        oper_im = laplace[1] + wave_rows[0][:, None] * pressure[1] + wave_rows[1][:, None] * pressure[0]
        shaped_re = oper_re.reshape(VERTICAL_GROUPS, BLK, AZ)
        shaped_im = oper_im.reshape(VERTICAL_GROUPS, BLK, AZ)
        zero_acc = jnp.zeros((VERTICAL_GROUPS, BLK, AZ), jnp.float32)
        increment, unused = lax.scan(partial(solve_term, shaped_re=shaped_re, shaped_im=shaped_im), (zero_acc, zero_acc), term_inputs)
        moved_re = pressure[0] + increment[0].reshape(DEPTH, AZ)
        moved_im = pressure[1] + increment[1].reshape(DEPTH, AZ)
        spectrum = jnp.fft.fft(lax.complex(moved_re, moved_im), axis=1) * turn
        spatial_field = jnp.fft.ifft(spectrum, axis=1)
        pressure = jnp.stack([jnp.real(spatial_field), jnp.imag(spatial_field)]) * damping[None]
    return pressure
```

```python
import math

import jax
import jax.numpy as jnp
import numpy as np
from jax import lax
from jax.experimental import pallas as pl
from jax.experimental.pallas import tpu as pltpu
from jax.sharding import PartitionSpec as P

STEPS = 2
LANES = 128
VMEM_BYTES = 48 * 1024 * 1024


def split(value):
    high = value.astype(jnp.bfloat16)
    low = (value - high.astype(jnp.float32)).astype(jnp.bfloat16)
    return high, low


def dot_split(left, right):
    def one(a, b):
        return jnp.dot(a, b, preferred_element_type=jnp.float32)

    return one(left[0], right[0]) + (one(left[0], right[1]) + one(left[1], right[0]))


def mul(a, b):
    return (a[0] * b[0] - a[1] * b[1], a[0] * b[1] + a[1] * b[0])


def sub(a, b):
    return (a[0] - b[0], a[1] - b[1])


def add(a, b):
    return (a[0] + b[0], a[1] + b[1])


def small_dft(values, sign):
    count = len(values)
    if count == 1:
        return values
    even = small_dft(values[0::2], sign)
    odd = small_dft(values[1::2], sign)
    half = count // 2
    low, high = [], []
    for k in range(half):
        re, im = odd[k]
        if k == 0:
            turned = (re, im)
        elif 4 * k == count:
            turned = (-sign * im, sign * re) if sign > 0 else (im, -re)
        elif 8 * k == count:
            root = math.sqrt(0.5)
            turned = ((re - sign * im) * root, (im + sign * re) * root)
        elif 8 * k == 3 * count:
            root = math.sqrt(0.5)
            turned = ((-re - sign * im) * root, (sign * re - im) * root)
        else:
            angle = 2.0 * math.pi * k / count
            turned = mul((re, im), (math.cos(angle), sign * math.sin(angle)))
        low.append(add(even[k], turned))
        high.append(sub(even[k], turned))
    return low + high


def cos_sin(x):
    turns = jnp.floor(x * (2.0 / math.pi) + 0.5)
    r = ((x - turns * 1.5703125) - turns * 4.837512969970703e-4) - turns * 7.549789948768648e-08
    q = turns.astype(jnp.int32)
    s = r * r
    sin_r = r + r * s * (-1.6666654611e-1 + s * (8.3321608736e-3 + s * -1.9515295891e-4))
    cos_r = (1.0 - 0.5 * s) + s * s * (
        4.166664568298827e-2 + s * (-1.388731625493765e-3 + s * 2.443315711809948e-5)
    )
    swap = (q & 1) == 1
    cos_x = jnp.where(swap, sin_r, cos_r)
    sin_x = jnp.where(swap, cos_r, sin_r)
    cos_x = jnp.where(((q + 1) & 2) == 2, -cos_x, cos_x)
    sin_x = jnp.where((q & 2) == 2, -sin_x, sin_x)
    return cos_x, sin_x


def parts8(rows):
    return (rows[0:8], rows[8:16])


def depth_kernel(wave_ref, p_ref, halo_ref, g_ref, col_ref, y_ref, ends_ref, sum_ref):
    blocks, block_rows = g_ref.shape[0], g_ref.shape[2] // 2
    chunk_rows = p_ref.shape[2]
    per = block_rows // chunk_rows
    lane_count = p_ref.shape[3]

    def block_of(part, b):
        return jnp.concatenate([p_ref[b * per + i, part] for i in range(per)], axis=0)

    firsts, lasts = [], []
    for b in range(blocks):
        own = [block_of(0, b), block_of(1, b)]
        lap = []
        for part in range(2):
            if b == 0:
                above = halo_ref[0, part : part + 1]
            else:
                above = p_ref[b * per - 1, part, chunk_rows - 1 : chunk_rows]
            if b == blocks - 1:
                below = halo_ref[1, part : part + 1]
            else:
                below = p_ref[(b + 1) * per, part, 0:1]
            up = jnp.concatenate([above, own[part][:-1]], axis=0)
            down = jnp.concatenate([own[part][1:], below], axis=0)
            lap.append(up + down - 2.0 * own[part])
        w_re, w_im = wave_ref[0, b], wave_ref[1, b]
        x = jnp.concatenate(
            [
                lap[0] + w_re * own[0] - w_im * own[1],
                lap[1] + w_re * own[1] + w_im * own[0],
            ],
            axis=0,
        )
        out = dot_split(split(g_ref[b]), split(x))
        for part in range(2):
            moved = own[part] + out[part * block_rows : (part + 1) * block_rows]
            for i in range(per):
                y_ref[b * per + i, part] = moved[i * chunk_rows : (i + 1) * chunk_rows]
        ends = out[2 * block_rows :]
        ends_ref[b] = ends
        firsts.append(parts8(ends[0:16]))
        lasts.append(parts8(ends[16:32]))
    zero = jnp.zeros((8, lane_count), jnp.float32)
    s = (zero, zero)
    heads = []
    for b in range(blocks):
        heads.append(sub(firsts[b], mul((col_ref[b, 2], col_ref[b, 3]), s)))
        s = sub(lasts[b], mul((col_ref[b, 0], col_ref[b, 1]), s))
    t = (zero, zero)
    for b in reversed(range(blocks)):
        t = sub(heads[b], mul((col_ref[b, 4], col_ref[b, 5]), t))
    sum_ref[...] = jnp.concatenate([s[0], s[1], t[0], t[1]], axis=0)


def link_kernel(here_ref, y_ref, ends_ref, sums_ref, col_ref, c_ref, out_ref):
    blocks = ends_ref.shape[0]
    devices = sums_ref.shape[0]
    chunk_rows = y_ref.shape[2]
    block_rows = c_ref.shape[1] // 2
    per = block_rows // chunk_rows
    here = here_ref[0]
    zero = jnp.zeros((8, y_ref.shape[3]), jnp.float32)

    def lam(b):
        return (col_ref[b, 0], col_ref[b, 1])

    def mu(b):
        return (col_ref[b, 2], col_ref[b, 3])

    def ups(b):
        return (col_ref[b, 4], col_ref[b, 5])

    entering = []
    s = (zero, zero)
    for d in range(devices):
        entering.append(s)
        if d < devices - 1:
            carried = s
            for b in range(d * blocks, (d + 1) * blocks):
                pair = mul(lam(b), carried)
                carried = (-pair[0], -pair[1])
            s = add(carried, parts8(sums_ref[d, 0:16]))
    leaving = [None] * devices
    t = (zero, zero)
    for d in reversed(range(devices)):
        leaving[d] = t
        if d > 0:
            carried = entering[d]
            heads = []
            for b in range(d * blocks, (d + 1) * blocks):
                pair = mul(mu(b), carried)
                heads.append((-pair[0], -pair[1]))
                pair = mul(lam(b), carried)
                carried = (-pair[0], -pair[1])
            back = t
            for b in reversed(range(d * blocks, (d + 1) * blocks)):
                back = sub(heads[b - d * blocks], mul(ups(b), back))
            t = add(back, parts8(sums_ref[d, 16:32]))
    s, t = entering[0], leaving[0]
    for d in range(1, devices):
        s = tuple(jnp.where(here == d, a, b) for a, b in zip(entering[d], s))
        t = tuple(jnp.where(here == d, a, b) for a, b in zip(leaving[d], t))

    def mine(b, k):
        return (col_ref[here * blocks + b, k], col_ref[here * blocks + b, k + 1])

    s_in, heads = [], []
    for b in range(blocks):
        s_in.append(s)
        first, last = parts8(ends_ref[b, 0:16]), parts8(ends_ref[b, 16:32])
        heads.append(sub(first, mul(mine(b, 2), s)))
        s = sub(last, mul(mine(b, 0), s))
    t_in = [None] * blocks
    for b in reversed(range(blocks)):
        t_in[b] = t
        t = sub(heads[b], mul(mine(b, 4), t))
    for b in range(blocks):
        carry = jnp.concatenate([s_in[b][0], s_in[b][1], t_in[b][0], t_in[b][1]], axis=0)
        fix = dot_split(split(c_ref[b]), split(carry))
        for part in range(2):
            for i in range(per):
                low = part * block_rows + i * chunk_rows
                out_ref[b * per + i, part] = y_ref[b * per + i, part] + fix[low : low + chunk_rows]


def azimuth_kernel(
    x_ref, c_ref, spatial_ref, twist_ref, fwd_ref, inv_ref, damp_ref, out_ref, held
):
    sources, rows, lane_count = x_ref.shape[0], x_ref.shape[2], x_ref.shape[3]
    tiles = lane_count // LANES
    outer = sources * tiles

    def where(a):
        return a // tiles, pl.ds((a % tiles) * LANES, LANES)

    @pl.loop(0, rows // 8)
    def _(g):
        at = pl.ds(pl.multiple_of(g * 8, 8), 8)
        values = []
        for a in range(outer):
            src, lanes = where(a)
            values.append((x_ref[src, 0, at, lanes], x_ref[src, 1, at, lanes]))
        for k, value in enumerate(small_dft(values, -1)):
            turned = mul(value, (twist_ref[0, k : k + 1], twist_ref[1, k : k + 1]))
            held[k, at, 0:LANES] = turned[0]
            held[k, at, LANES:] = turned[1]

    fwd = split(fwd_ref[...])
    inv = split(inv_ref[...])
    group = 4

    @pl.loop(0, outer // group)
    def _(g):
        at = pl.ds(g * group, group)
        x = held[at].reshape(group * rows, 2 * LANES)
        spec = dot_split(split(x), fwd).reshape(group, rows, 2 * LANES)
        turn_re, turn_im = cos_sin(c_ref[...][None] * spatial_ref[at])
        re, im = spec[..., :LANES], spec[..., LANES:]
        y = jnp.concatenate([re * turn_re + im * turn_im, im * turn_re - re * turn_im], axis=2)
        held[at] = dot_split(split(y.reshape(group * rows, 2 * LANES)), inv).reshape(
            group, rows, 2 * LANES
        )

    @pl.loop(0, rows // 8)
    def _(g):
        at = pl.ds(pl.multiple_of(g * 8, 8), 8)
        values = []
        for k in range(outer):
            value = (held[k, at, 0:LANES], held[k, at, LANES:])
            values.append(mul(value, (twist_ref[0, k : k + 1], -twist_ref[1, k : k + 1])))
        for a, value in enumerate(small_dft(values, 1)):
            src, lanes = where(a)
            damp = damp_ref[a : a + 1]
            out_ref[src, 0, at, lanes] = value[0] * damp
            out_ref[src, 1, at, lanes] = value[1] * damp


def tables(total):
    outer = total // LANES
    k1 = np.arange(outer)[:, None]
    a2 = np.arange(LANES)[None, :]
    angle = 2.0 * np.pi * ((k1 * a2) % total) / total
    twist = np.stack([np.cos(angle), -np.sin(angle)])
    angle = 2.0 * np.pi * ((np.arange(LANES)[:, None] * a2) % LANES) / LANES
    cos, sin = np.cos(angle), np.sin(angle)
    fwd = np.block([[cos, -sin], [sin, cos]])
    inv = np.block([[cos, sin], [-sin, cos]]) / total
    k = k1 + outer * a2
    signed = np.where(k < total // 2, k, k - total)
    spatial = ((2.0 * np.pi * signed / total) ** 2)[:, None, :]
    return [value.astype(np.float32) for value in (spatial, twist, fwd, inv)]


def vmem(count):
    return [pl.BlockSpec(memory_space=pltpu.VMEM)] * count


def smem():
    return pl.BlockSpec(memory_space=pltpu.SMEM)


def params():
    return pltpu.CompilerParams(vmem_limit_bytes=VMEM_BYTES)


def f32(*shape):
    return jax.ShapeDtypeStruct(shape, jnp.float32)


def weighted(inverses, lower, upper, weights):
    w_re, w_im = weights[0], weights[1]

    def total(re, im):
        shape = (-1,) + (1,) * (re.ndim - 1)
        a, b = w_re.reshape(shape), w_im.reshape(shape)
        return a * re - b * im, a * im + b * re

    m_re, m_im = total(inverses[0], inverses[1])
    m_re, m_im = m_re.sum(0), m_im.sum(0)

    def real_rows(re, im):
        return [jnp.concatenate([re, -im], axis=-1), jnp.concatenate([im, re], axis=-1)]

    first = jnp.moveaxis(inverses[:, :, :, 0], 1, 2)
    last = jnp.moveaxis(inverses[:, :, :, -1], 1, 2)
    g = jnp.concatenate(
        real_rows(m_re, m_im) + real_rows(first[0], first[1]) + real_rows(last[0], last[1]), axis=1
    )
    wl_re, wl_im = (jnp.transpose(v, (1, 2, 0)) for v in total(lower[0], lower[1]))
    wu_re, wu_im = (jnp.transpose(v, (1, 2, 0)) for v in total(upper[0], upper[1]))
    c = jnp.concatenate(
        [
            jnp.concatenate([-wl_re, wl_im, -wu_re, wu_im], axis=-1),
            jnp.concatenate([-wl_im, -wl_re, -wu_im, -wu_re], axis=-1),
        ],
        axis=1,
    )
    return g, c


def local(
    pressure_field,
    block_inverses,
    lower_spikes,
    upper_spikes,
    pade_weights,
    layer_wavenumber,
    layer_index,
    depth_coupling,
    attenuation,
    sediment_type,
):
    parts, depth_rows, az_count = pressure_field.shape
    blocks, block_rows = block_inverses.shape[2], block_inverses.shape[3]
    n_az, n_depth = lax.axis_size("az"), lax.axis_size("depth")
    chunk = depth_rows // n_az
    total = n_az * az_count
    outer = total // LANES
    az_at = lax.axis_index("az")
    spatial, twist, fwd, inv = (jnp.asarray(v) for v in tables(total))
    g, c = weighted(block_inverses, lower_spikes, upper_spikes, pade_weights)
    terms = pade_weights.shape[1]
    columns = jnp.stack(
        [
            lower_spikes[0, :, :, -1],
            lower_spikes[1, :, :, -1],
            lower_spikes[0, :, :, 0],
            lower_spikes[1, :, :, 0],
            upper_spikes[0, :, :, 0],
            upper_spikes[1, :, :, 0],
        ]
    )
    columns = jnp.transpose(columns, (2, 0, 1))
    all_columns = lax.all_gather(columns, "depth").reshape(n_depth * blocks, 6, terms, 1)
    columns = columns.reshape(blocks, 6, terms, 1)
    wave = layer_wavenumber[:, layer_index]
    types = lax.all_gather(sediment_type, "az", tiled=True)
    layer = lax.dynamic_index_in_dim(layer_index, az_at * chunk // block_rows, keepdims=False)
    fade = lax.dynamic_index_in_dim(attenuation, layer, keepdims=False)
    exponent = jnp.zeros(types.shape, jnp.float32)
    for kind in range(attenuation.shape[1]):
        exponent = jnp.where(types == kind, fade[kind], exponent)
    damp = jnp.exp(-exponent).reshape(outer, LANES)
    coupling = lax.dynamic_slice_in_dim(depth_coupling, az_at * chunk, chunk).reshape(chunk, 1)
    here = lax.axis_index("depth").astype(jnp.int32).reshape(1)
    grid_shape = (n_az, parts, chunk, az_count)
    field = jnp.transpose(pressure_field.reshape(parts, n_az, chunk, az_count), (1, 0, 2, 3))
    down = [(i, i + 1) for i in range(n_depth - 1)]
    up = [(i + 1, i) for i in range(n_depth - 1)]
    for _ in range(STEPS):
        halo = jnp.stack(
            [
                lax.ppermute(field[-1, :, -1], "depth", down),
                lax.ppermute(field[0, :, 0], "depth", up),
            ]
        )
        y, ends, sums = pl.pallas_call(
            depth_kernel,
            out_shape=(
                f32(*grid_shape),
                f32(blocks, 4 * terms, az_count),
                f32(4 * terms, az_count),
            ),
            in_specs=[smem()] + vmem(4),
            out_specs=tuple(vmem(3)),
            compiler_params=params(),
            name="depth_solve",
        )(wave, field, halo, g, columns)
        all_sums = lax.all_gather(sums, "depth")
        advanced = pl.pallas_call(
            link_kernel,
            out_shape=f32(*grid_shape),
            in_specs=[smem()] + vmem(5),
            out_specs=vmem(1)[0],
            compiler_params=params(),
            name="depth_link",
        )(here, y, ends, all_sums, all_columns, c)
        lines = lax.all_to_all(advanced, "az", split_axis=0, concat_axis=0, tiled=True)
        coupled = pl.pallas_call(
            azimuth_kernel,
            out_shape=f32(*grid_shape),
            in_specs=vmem(7),
            out_specs=vmem(1)[0],
            scratch_shapes=[pltpu.VMEM((outer, chunk, 2 * LANES), jnp.float32)],
            compiler_params=params(),
            name="azimuth_couple",
        )(lines, coupling, spatial, twist, fwd, inv, damp)
        field = lax.all_to_all(coupled, "az", split_axis=0, concat_axis=0, tiled=True)
    return jnp.transpose(field, (1, 0, 2, 3)).reshape(parts, depth_rows, az_count)


def solution(mesh):
    in_specs = (
        P(None, "depth", "az"),
        P(None, None, "depth", None, None),
        P(None, None, "depth", None),
        P(None, None, "depth", None),
        P(),
        P(),
        P("depth"),
        P("depth"),
        P(),
        P("az"),
    )
    out_specs = P(None, "depth", "az")
    return jax.shard_map(local, mesh=mesh, in_specs=in_specs, out_specs=out_specs, check_vma=False)
```

```python
import functools
import math

import jax
import jax.numpy as jnp
import numpy as np
from jax import lax
from jax.experimental import pallas as pl
from jax.experimental.pallas import tpu as pltpu
from jax.sharding import PartitionSpec as P

STEPS = 2
LANES = 128
VMEM_BYTES = 48 * 1024 * 1024


def split(value):
    high = value.astype(jnp.bfloat16)
    low = (value - high.astype(jnp.float32)).astype(jnp.bfloat16)
    return high, low


def dot_split(left, right):
    def one(a, b):
        return jnp.dot(a, b, preferred_element_type=jnp.float32)

    return one(left[0], right[0]) + (one(left[0], right[1]) + one(left[1], right[0]))


def mul(a, b):
    return (a[0] * b[0] - a[1] * b[1], a[0] * b[1] + a[1] * b[0])


def sub(a, b):
    return (a[0] - b[0], a[1] - b[1])


def add(a, b):
    return (a[0] + b[0], a[1] + b[1])


def small_dft(values, sign):
    count = len(values)
    if count == 1:
        return values
    even = small_dft(values[0::2], sign)
    odd = small_dft(values[1::2], sign)
    half = count // 2
    low, high = [], []
    for k in range(half):
        re, im = odd[k]
        if k == 0:
            turned = (re, im)
        elif 4 * k == count:
            turned = (-sign * im, sign * re) if sign > 0 else (im, -re)
        elif 8 * k == count:
            root = math.sqrt(0.5)
            turned = ((re - sign * im) * root, (im + sign * re) * root)
        elif 8 * k == 3 * count:
            root = math.sqrt(0.5)
            turned = ((-re - sign * im) * root, (sign * re - im) * root)
        else:
            angle = 2.0 * math.pi * k / count
            turned = mul((re, im), (math.cos(angle), sign * math.sin(angle)))
        low.append(add(even[k], turned))
        high.append(sub(even[k], turned))
    return low + high


def cos_sin(x):
    turns = jnp.floor(x * (2.0 / math.pi) + 0.5)
    r = ((x - turns * 1.5703125) - turns * 4.837512969970703e-4) - turns * 7.549789948768648e-08
    q = turns.astype(jnp.int32)
    s = r * r
    sin_r = r + r * s * (-1.6666654611e-1 + s * (8.3321608736e-3 + s * -1.9515295891e-4))
    cos_r = (1.0 - 0.5 * s) + s * s * (
        4.166664568298827e-2 + s * (-1.388731625493765e-3 + s * 2.443315711809948e-5)
    )
    swap = (q & 1) == 1
    cos_x = jnp.where(swap, sin_r, cos_r)
    sin_x = jnp.where(swap, cos_r, sin_r)
    cos_x = jnp.where(((q + 1) & 2) == 2, -cos_x, cos_x)
    sin_x = jnp.where((q & 2) == 2, -sin_x, sin_x)
    return cos_x, sin_x


def parts8(rows):
    return (rows[0:8], rows[8:16])


def depth_kernel(wave_ref, p_ref, halo_ref, g_ref, col_ref, y_ref, ends_ref, sum_ref):
    blocks, block_rows = g_ref.shape[0], g_ref.shape[2] // 2
    chunk_rows = p_ref.shape[2]
    per = block_rows // chunk_rows
    lane_count = p_ref.shape[3]

    def block_of(part, b):
        return jnp.concatenate([p_ref[b * per + i, part] for i in range(per)], axis=0)

    firsts, lasts = [], []
    for b in range(blocks):
        own = [block_of(0, b), block_of(1, b)]
        lap = []
        for part in range(2):
            if b == 0:
                above = halo_ref[0, part : part + 1]
            else:
                above = p_ref[b * per - 1, part, chunk_rows - 1 : chunk_rows]
            if b == blocks - 1:
                below = halo_ref[1, part : part + 1]
            else:
                below = p_ref[(b + 1) * per, part, 0:1]
            up = jnp.concatenate([above, own[part][:-1]], axis=0)
            down = jnp.concatenate([own[part][1:], below], axis=0)
            lap.append(up + down - 2.0 * own[part])
        w_re, w_im = wave_ref[0, b], wave_ref[1, b]
        x = jnp.concatenate(
            [
                lap[0] + w_re * own[0] - w_im * own[1],
                lap[1] + w_re * own[1] + w_im * own[0],
            ],
            axis=0,
        )
        out = dot_split(split(g_ref[b]), split(x))
        for part in range(2):
            moved = own[part] + out[part * block_rows : (part + 1) * block_rows]
            for i in range(per):
                y_ref[b * per + i, part] = moved[i * chunk_rows : (i + 1) * chunk_rows]
        ends = out[2 * block_rows :]
        ends_ref[b] = ends
        firsts.append(parts8(ends[0:16]))
        lasts.append(parts8(ends[16:32]))
    zero = jnp.zeros((8, lane_count), jnp.float32)
    s = (zero, zero)
    heads = []
    for b in range(blocks):
        heads.append(sub(firsts[b], mul((col_ref[b, 2], col_ref[b, 3]), s)))
        s = sub(lasts[b], mul((col_ref[b, 0], col_ref[b, 1]), s))
    t = (zero, zero)
    for b in reversed(range(blocks)):
        t = sub(heads[b], mul((col_ref[b, 4], col_ref[b, 5]), t))
    sum_ref[...] = jnp.concatenate([s[0], s[1], t[0], t[1]], axis=0)


def link_kernel(here_ref, y_ref, ends_ref, sums_ref, col_ref, c_ref, out_ref):
    blocks = ends_ref.shape[0]
    devices = sums_ref.shape[0]
    chunk_rows = y_ref.shape[2]
    block_rows = c_ref.shape[1] // 2
    per = block_rows // chunk_rows
    here = here_ref[0]
    zero = jnp.zeros((8, y_ref.shape[3]), jnp.float32)

    def lam(b):
        return (col_ref[b, 0], col_ref[b, 1])

    def mu(b):
        return (col_ref[b, 2], col_ref[b, 3])

    def ups(b):
        return (col_ref[b, 4], col_ref[b, 5])

    entering = []
    s = (zero, zero)
    for d in range(devices):
        entering.append(s)
        if d < devices - 1:
            carried = s
            for b in range(d * blocks, (d + 1) * blocks):
                pair = mul(lam(b), carried)
                carried = (-pair[0], -pair[1])
            s = add(carried, parts8(sums_ref[d, 0:16]))
    leaving = [None] * devices
    t = (zero, zero)
    for d in reversed(range(devices)):
        leaving[d] = t
        if d > 0:
            carried = entering[d]
            heads = []
            for b in range(d * blocks, (d + 1) * blocks):
                pair = mul(mu(b), carried)
                heads.append((-pair[0], -pair[1]))
                pair = mul(lam(b), carried)
                carried = (-pair[0], -pair[1])
            back = t
            for b in reversed(range(d * blocks, (d + 1) * blocks)):
                back = sub(heads[b - d * blocks], mul(ups(b), back))
            t = add(back, parts8(sums_ref[d, 16:32]))
    s, t = entering[0], leaving[0]
    for d in range(1, devices):
        s = tuple(jnp.where(here == d, a, b) for a, b in zip(entering[d], s))
        t = tuple(jnp.where(here == d, a, b) for a, b in zip(leaving[d], t))

    def mine(b, k):
        return (col_ref[here * blocks + b, k], col_ref[here * blocks + b, k + 1])

    s_in, heads = [], []
    for b in range(blocks):
        s_in.append(s)
        first, last = parts8(ends_ref[b, 0:16]), parts8(ends_ref[b, 16:32])
        heads.append(sub(first, mul(mine(b, 2), s)))
        s = sub(last, mul(mine(b, 0), s))
    t_in = [None] * blocks
    for b in reversed(range(blocks)):
        t_in[b] = t
        t = sub(heads[b], mul(mine(b, 4), t))
    for b in range(blocks):
        carry = jnp.concatenate([s_in[b][0], s_in[b][1], t_in[b][0], t_in[b][1]], axis=0)
        fix = dot_split(split(c_ref[b]), split(carry))
        for part in range(2):
            for i in range(per):
                low = part * block_rows + i * chunk_rows
                out_ref[b * per + i, part] = y_ref[b * per + i, part] + fix[low : low + chunk_rows]


def azimuth_kernel(
    x_ref, c_ref, spatial_ref, twist_ref, fwd_ref, inv_ref, damp_ref, out_ref, edge_ref, held
):
    sources, rows, lane_count = x_ref.shape[0], x_ref.shape[2], x_ref.shape[3]
    tiles = lane_count // LANES
    outer = sources * tiles

    def where(a):
        return a // tiles, pl.ds((a % tiles) * LANES, LANES)

    @pl.loop(0, rows // 8)
    def _(g):
        at = pl.ds(pl.multiple_of(g * 8, 8), 8)
        values = []
        for a in range(outer):
            src, lanes = where(a)
            values.append((x_ref[src, 0, at, lanes], x_ref[src, 1, at, lanes]))
        for k, value in enumerate(small_dft(values, -1)):
            turned = mul(value, (twist_ref[0, k : k + 1], twist_ref[1, k : k + 1]))
            held[k, at, 0:LANES] = turned[0]
            held[k, at, LANES:] = turned[1]

    fwd = split(fwd_ref[...])
    inv = split(inv_ref[...])
    group = 4

    @pl.loop(0, outer // group)
    def _(g):
        at = pl.ds(g * group, group)
        x = held[at].reshape(group * rows, 2 * LANES)
        spec = dot_split(split(x), fwd).reshape(group, rows, 2 * LANES)
        turn_re, turn_im = cos_sin(c_ref[...][None] * spatial_ref[at])
        re, im = spec[..., :LANES], spec[..., LANES:]
        y = jnp.concatenate([re * turn_re + im * turn_im, im * turn_re - re * turn_im], axis=2)
        held[at] = dot_split(split(y.reshape(group * rows, 2 * LANES)), inv).reshape(
            group, rows, 2 * LANES
        )

    @pl.loop(0, rows // 8)
    def _(g):
        at = pl.ds(pl.multiple_of(g * 8, 8), 8)
        values = []
        for k in range(outer):
            value = (held[k, at, 0:LANES], held[k, at, LANES:])
            values.append(mul(value, (twist_ref[0, k : k + 1], -twist_ref[1, k : k + 1])))
        for a, value in enumerate(small_dft(values, 1)):
            src, lanes = where(a)
            damp = damp_ref[a : a + 1]
            out_ref[src, 0, at, lanes] = value[0] * damp
            out_ref[src, 1, at, lanes] = value[1] * damp

    for part in range(2):
        for src in range(sources):
            row = pl.ds(part * sources + src, 1)
            edge_ref[0, row] = out_ref[src, part, 0:1]
            edge_ref[1, row] = out_ref[src, part, rows - 1 : rows]


def tables(total):
    outer = total // LANES
    k1 = np.arange(outer)[:, None]
    a2 = np.arange(LANES)[None, :]
    angle = 2.0 * np.pi * ((k1 * a2) % total) / total
    twist = np.stack([np.cos(angle), -np.sin(angle)])
    angle = 2.0 * np.pi * ((np.arange(LANES)[:, None] * a2) % LANES) / LANES
    cos, sin = np.cos(angle), np.sin(angle)
    fwd = np.block([[cos, -sin], [sin, cos]])
    inv = np.block([[cos, sin], [-sin, cos]]) / total
    k = k1 + outer * a2
    signed = np.where(k < total // 2, k, k - total)
    spatial = ((2.0 * np.pi * signed / total) ** 2)[:, None, :]
    return [value.astype(np.float32) for value in (spatial, twist, fwd, inv)]


MESH_IDS = pl.DeviceIdType.MESH


def greet(devices):
    barrier = pltpu.get_barrier_semaphore()
    for present, device in devices:

        def tell(device=device):
            pl.semaphore_signal(barrier, inc=1, device_id=device, device_id_type=MESH_IDS)

        if present is None:
            tell()
        else:
            pl.when(present)(tell)
    amount = 0
    for present, _ in devices:
        amount = amount + (1 if present is None else jnp.where(present, 1, 0))
    pl.semaphore_wait(barrier, amount)


def remote(src, dst, send, recv, device):
    return pltpu.make_async_remote_copy(
        src_ref=src,
        dst_ref=dst,
        send_sem=send,
        recv_sem=recv,
        device_id=device,
        device_id_type=MESH_IDS,
    )


def exchange_kernel(forward, n, src_ref, dst_ref, send_sem, recv_sem):
    depth, az = lax.axis_index("depth"), lax.axis_index("az")
    pair, core = depth // 2, depth % 2
    half = n // 2
    peers = []
    for step in range(1, 2 * n):
        other = (core * n + az + step) % (2 * n)
        peers.append((None, (2 * pair + other // n, other % n)))
    greet(peers)
    moves = []
    for step in range(n):
        j = (step + az) % n
        if forward:
            device = (2 * pair + j % 2, half * core + j // 2)
            slot = az
        else:
            device = (2 * pair + az // half, j)
            slot = 2 * (az % half) + core
        away = jnp.logical_or(device[0] != depth, device[1] != az)
        move = remote(src_ref.at[j], dst_ref.at[slot], send_sem.at[step], recv_sem.at[slot], device)
        stay = pltpu.make_async_copy(src_ref.at[j], dst_ref.at[slot], recv_sem.at[slot])
        pl.when(away)(move.start)
        pl.when(jnp.logical_not(away))(stay.start)
        moves.append((away, move))
    for slot in range(n):
        pltpu.make_async_copy(src_ref.at[slot], dst_ref.at[slot], recv_sem.at[slot]).wait()
    for away, move in moves:
        pl.when(away)(move.wait_send)


def exchange(value, forward):
    n = value.shape[0]
    return pl.pallas_call(
        functools.partial(exchange_kernel, forward, n),
        out_shape=jax.ShapeDtypeStruct(value.shape, value.dtype),
        in_specs=[pl.BlockSpec(memory_space=pl.ANY)],
        out_specs=pl.BlockSpec(memory_space=pl.ANY),
        scratch_shapes=[pltpu.SemaphoreType.DMA((n,)), pltpu.SemaphoreType.DMA((n,))],
        compiler_params=pltpu.CompilerParams(
            collective_id=0 if forward else 1, has_side_effects=True
        ),
        name="exchange_out" if forward else "exchange_back",
    )(value)


def neighbour_kernel(n, total_blocks, own_ref, edge_ref, other_ref, halo_ref, send_sem, recv_sem):
    depth, az = lax.axis_index("depth"), lax.axis_index("az")
    pair, core = depth // 2, depth % 2
    block = pair * n + az
    partner = (2 * pair + 1 - core, az)
    above, below = block > 0, block < total_blocks - 1

    def at(b, c):
        return (2 * (b // n) + c, b % n)

    greet(
        [(None, partner)]
        + [(above, at(block - 1, c)) for c in range(2)]
        + [(below, at(block + 1, c)) for c in range(2)]
    )
    whole = remote(own_ref, other_ref, send_sem.at[0], recv_sem.at[0], partner)
    whole.start()
    sends = []
    for c in range(2):
        sends.append(
            (
                jnp.logical_and(below, core == 1),
                remote(
                    edge_ref.at[1], halo_ref.at[0], send_sem.at[1 + c], recv_sem.at[1], at(block + 1, c)
                ),
            )
        )
        sends.append(
            (
                jnp.logical_and(above, core == 0),
                remote(
                    edge_ref.at[0], halo_ref.at[1], send_sem.at[3 + c], recv_sem.at[2], at(block - 1, c)
                ),
            )
        )
    for present, move in sends:
        pl.when(present)(move.start)
    for side, present in ((0, above), (1, below)):
        got = pltpu.make_async_copy(edge_ref.at[side], halo_ref.at[side], recv_sem.at[1 + side])
        pl.when(present)(got.wait)

        @pl.when(jnp.logical_not(present))
        def _(side=side):
            halo_ref[side] = jnp.zeros(halo_ref.shape[1:], jnp.float32)

    for present, move in sends:
        pl.when(present)(move.wait_send)
    whole.wait()


def neighbours(field, edge, total_blocks):
    n = field.shape[0]
    return pl.pallas_call(
        functools.partial(neighbour_kernel, n, total_blocks),
        out_shape=(f32(*field.shape), f32(*edge.shape)),
        in_specs=[pl.BlockSpec(memory_space=pl.ANY), pl.BlockSpec(memory_space=pltpu.VMEM)],
        out_specs=(pl.BlockSpec(memory_space=pl.ANY), pl.BlockSpec(memory_space=pltpu.VMEM)),
        scratch_shapes=[pltpu.SemaphoreType.DMA((5,)), pltpu.SemaphoreType.DMA((3,))],
        compiler_params=pltpu.CompilerParams(collective_id=2, has_side_effects=True),
        name="neighbours",
    )(field, edge)


def row_solve_kernel(wave_ref, core_ref, own_ref, other_ref, halo_ref, g_ref, y_ref, ends_ref):
    sources, chunk_rows, lane_count = own_ref.shape[0], own_ref.shape[2], own_ref.shape[3]
    tiles = lane_count // LANES
    first = core_ref[0] == 0
    g = split(g_ref[...])
    w_re, w_im = wave_ref[0], wave_ref[1]
    for src in range(sources):
        own, lap, mine = [], [], []
        for part in range(2):
            here, there = own_ref[src, part], other_ref[src, part]
            top, bottom = jnp.where(first, here, there), jnp.where(first, there, here)
            row = part * sources + src
            rows = jnp.concatenate([top, bottom], axis=0)
            up = jnp.concatenate([halo_ref[0, row : row + 1], rows[:-1]], axis=0)
            down = jnp.concatenate([rows[1:], halo_ref[1, row : row + 1]], axis=0)
            own.append(rows)
            mine.append(here)
            lap.append(up + down - 2.0 * rows)
        x = jnp.concatenate(
            [
                lap[0] + w_re * own[0] - w_im * own[1],
                lap[1] + w_re * own[1] + w_im * own[0],
            ],
            axis=0,
        )
        out = dot_split(g, split(x))
        y_ref[src, 0] = mine[0] + out[:chunk_rows]
        y_ref[src, 1] = mine[1] + out[chunk_rows : 2 * chunk_rows]
        for tile in range(tiles):
            ends_ref[src * tiles + tile] = out[2 * chunk_rows :, tile * LANES : (tile + 1) * LANES]


def sweep_kernel(n, count, ends_ref, col_ref, out_ref, got, answer, sem_a, sem_b, sem_c, sem_d, sem_e):
    depth, az = lax.axis_index("depth"), lax.axis_index("az")
    pair, core = depth // 2, depth % 2
    block = pair * n + az
    partner = (2 * pair + 1 - core, az)

    def at(b):
        return (2 * (b // n) + core, b % n)

    others = [(block + step) % count for step in range(1, count)]
    greet([(None, partner)] + [(None, at(b)) for b in others])
    base = core * count
    moves = [
        remote(ends_ref.at[base + b], got.at[block], sem_a.at[i], sem_b.at[block], at(b))
        for i, b in enumerate(others)
    ]
    for move in moves:
        move.start()
    pltpu.make_async_copy(ends_ref.at[base + block], got.at[block], sem_b.at[block]).start()
    for b in range(count):
        pltpu.make_async_copy(ends_ref.at[b], got.at[b], sem_b.at[b]).wait()
    for move in moves:
        move.wait_send()
    zero = jnp.zeros((8, LANES), jnp.float32)
    s = (zero, zero)
    heads = []
    for b in range(count):
        first, last = parts8(got[b, 0:16]), parts8(got[b, 16:32])
        answer[b, 0:8] = s[0]
        answer[b, 8:16] = s[1]
        heads.append(sub(first, mul((col_ref[b, 2], col_ref[b, 3]), s)))
        s = sub(last, mul((col_ref[b, 0], col_ref[b, 1]), s))
    t = (zero, zero)
    for b in reversed(range(count)):
        answer[b, 16:24] = t[0]
        answer[b, 24:32] = t[1]
        t = sub(heads[b], mul((col_ref[b, 4], col_ref[b, 5]), t))
    moves = [
        remote(answer.at[b], out_ref.at[base + block], sem_a.at[i], sem_c.at[block], at(b))
        for i, b in enumerate(others)
    ]
    for move in moves:
        move.start()
    pltpu.make_async_copy(answer.at[block], out_ref.at[base + block], sem_c.at[block]).start()
    for b in range(count):
        pltpu.make_async_copy(answer.at[b], out_ref.at[base + b], sem_c.at[b]).wait()
    for move in moves:
        move.wait_send()
    rows = out_ref.at[pl.ds(base, count)]
    swap = remote(rows, rows, sem_d.at[0], sem_e.at[0], partner)
    swap.start()
    swap.wait()


def sweeps(ends, columns, n):
    count = columns.shape[0]
    dma = pltpu.SemaphoreType.DMA
    return pl.pallas_call(
        functools.partial(sweep_kernel, n, count),
        out_shape=f32(*ends.shape),
        in_specs=vmem(2),
        out_specs=vmem(1)[0],
        scratch_shapes=[
            pltpu.VMEM((count, 32, LANES), jnp.float32),
            pltpu.VMEM((count, 32, LANES), jnp.float32),
            dma((count - 1,)),
            dma((count,)),
            dma((count,)),
            dma((1,)),
            dma((1,)),
        ],
        compiler_params=pltpu.CompilerParams(collective_id=3, has_side_effects=True),
        name="sweeps",
    )(ends, columns)


def row_link_kernel(y_ref, carry_ref, c_ref, out_ref):
    sources, chunk_rows, lane_count = y_ref.shape[0], y_ref.shape[2], y_ref.shape[3]
    tiles = lane_count // LANES
    c = split(c_ref[...])
    for src in range(sources):
        carry = jnp.concatenate([carry_ref[src * tiles + i] for i in range(tiles)], axis=1)
        fix = dot_split(c, split(carry))
        for part in range(2):
            out_ref[src, part] = y_ref[src, part] + fix[part * chunk_rows : (part + 1) * chunk_rows]


def vmem(count):
    return [pl.BlockSpec(memory_space=pltpu.VMEM)] * count


def smem():
    return pl.BlockSpec(memory_space=pltpu.SMEM)


def params():
    return pltpu.CompilerParams(vmem_limit_bytes=VMEM_BYTES)


def f32(*shape):
    return jax.ShapeDtypeStruct(shape, jnp.float32)


def weighted(inverses, lower, upper, weights):
    w_re, w_im = weights[0], weights[1]

    def total(re, im):
        shape = (-1,) + (1,) * (re.ndim - 1)
        a, b = w_re.reshape(shape), w_im.reshape(shape)
        return a * re - b * im, a * im + b * re

    m_re, m_im = total(inverses[0], inverses[1])
    m_re, m_im = m_re.sum(0), m_im.sum(0)

    def real_rows(re, im):
        return [jnp.concatenate([re, -im], axis=-1), jnp.concatenate([im, re], axis=-1)]

    first = jnp.moveaxis(inverses[:, :, :, 0], 1, 2)
    last = jnp.moveaxis(inverses[:, :, :, -1], 1, 2)
    g = jnp.concatenate(
        real_rows(m_re, m_im) + real_rows(first[0], first[1]) + real_rows(last[0], last[1]), axis=1
    )
    wl_re, wl_im = (jnp.transpose(v, (1, 2, 0)) for v in total(lower[0], lower[1]))
    wu_re, wu_im = (jnp.transpose(v, (1, 2, 0)) for v in total(upper[0], upper[1]))
    c = jnp.concatenate(
        [
            jnp.concatenate([-wl_re, wl_im, -wu_re, wu_im], axis=-1),
            jnp.concatenate([-wl_im, -wl_re, -wu_im, -wu_re], axis=-1),
        ],
        axis=1,
    )
    return g, c


def local(
    pressure_field,
    block_inverses,
    lower_spikes,
    upper_spikes,
    pade_weights,
    layer_wavenumber,
    layer_index,
    depth_coupling,
    attenuation,
    sediment_type,
):
    parts, depth_rows, az_count = pressure_field.shape
    blocks, block_rows = block_inverses.shape[2], block_inverses.shape[3]
    n_az, n_depth = lax.axis_size("az"), lax.axis_size("depth")
    chunk = depth_rows // n_az
    total = n_az * az_count
    outer = total // LANES
    az_at = lax.axis_index("az")
    spatial, twist, fwd, inv = (jnp.asarray(v) for v in tables(total))
    g, c = weighted(block_inverses, lower_spikes, upper_spikes, pade_weights)
    terms = pade_weights.shape[1]
    columns = jnp.stack(
        [
            lower_spikes[0, :, :, -1],
            lower_spikes[1, :, :, -1],
            lower_spikes[0, :, :, 0],
            lower_spikes[1, :, :, 0],
            upper_spikes[0, :, :, 0],
            upper_spikes[1, :, :, 0],
        ]
    )
    columns = jnp.transpose(columns, (2, 0, 1))
    all_columns = lax.all_gather(columns, "depth").reshape(n_depth * blocks, 6, terms, 1)
    columns = columns.reshape(blocks, 6, terms, 1)
    wave = layer_wavenumber[:, layer_index]
    types = lax.all_gather(sediment_type, "az", tiled=True)
    depth_at = lax.axis_index("depth")
    by_block = (
        n_az == 2 * blocks
        and n_depth % 2 == 0
        and 2 * chunk == block_rows
        and n_depth * n_az * LANES == total
    )
    if by_block:
        core = depth_at % 2
        picked = (
            lax.dynamic_index_in_dim(g, az_at % blocks, keepdims=False),
            lax.dynamic_index_in_dim(c, az_at % blocks, keepdims=False),
            lax.dynamic_slice_in_dim(layer_index, az_at % blocks, 1),
            lax.dynamic_slice_in_dim(depth_coupling, az_at % blocks * block_rows, block_rows),
        )
        swap = [(i, i + 1 - 2 * (i % 2)) for i in range(n_depth)]
        other = jax.tree.map(lambda v: lax.ppermute(v, "depth", swap), picked)
        mine = core == az_at // blocks
        g_row, c_row, layer, coupling = jax.tree.map(
            lambda a, b: jnp.where(mine, a, b), picked, other
        )
        layer = layer[0]

        def half(value, start):
            return lax.dynamic_slice_in_dim(value, start + core * chunk, chunk)

        g_row = jnp.concatenate([half(g_row, 0), half(g_row, block_rows), g_row[2 * block_rows :]])
        c_row = jnp.concatenate([half(c_row, 0), half(c_row, block_rows)])
        coupling = half(coupling, 0).reshape(chunk, 1)
        row_wave = lax.dynamic_index_in_dim(layer_wavenumber, layer, axis=1, keepdims=False)
    else:
        layer = lax.dynamic_index_in_dim(layer_index, az_at * chunk // block_rows, keepdims=False)
        coupling = lax.dynamic_slice_in_dim(depth_coupling, az_at * chunk, chunk).reshape(chunk, 1)
    fade = lax.dynamic_index_in_dim(attenuation, layer, keepdims=False)
    exponent = jnp.zeros(types.shape, jnp.float32)
    for kind in range(attenuation.shape[1]):
        exponent = jnp.where(types == kind, fade[kind], exponent)
    damp = jnp.exp(-exponent).reshape(outer, LANES)
    here = lax.axis_index("depth").astype(jnp.int32).reshape(1)
    grid_shape = (n_az, parts, chunk, az_count)
    field = jnp.transpose(pressure_field.reshape(parts, n_az, chunk, az_count), (1, 0, 2, 3))
    down = [(i, i + 1) for i in range(n_depth - 1)]
    up = [(i + 1, i) for i in range(n_depth - 1)]

    def slab_solve(field, ready):
        halo = jnp.stack(
            [
                lax.ppermute(field[-1, :, -1], "depth", down),
                lax.ppermute(field[0, :, 0], "depth", up),
            ]
        )
        y, ends, sums = pl.pallas_call(
            depth_kernel,
            out_shape=(
                f32(*grid_shape),
                f32(blocks, 4 * terms, az_count),
                f32(4 * terms, az_count),
            ),
            in_specs=[smem()] + vmem(4),
            out_specs=tuple(vmem(3)),
            compiler_params=params(),
            name="depth_solve",
        )(wave, field, halo, g, columns)
        all_sums = lax.all_gather(sums, "depth")
        y, ready = lax.optimization_barrier((y, ready))
        advanced = pl.pallas_call(
            link_kernel,
            out_shape=f32(*grid_shape),
            in_specs=[smem()] + vmem(5),
            out_specs=vmem(1)[0],
            compiler_params=params(),
            name="depth_link",
        )(here, y, ends, all_sums, all_columns, c)
        return advanced, ready

    def couple(lines):
        return pl.pallas_call(
            azimuth_kernel,
            out_shape=(f32(*grid_shape), f32(2, parts * n_az, az_count)),
            in_specs=vmem(7),
            out_specs=tuple(vmem(2)),
            scratch_shapes=[pltpu.VMEM((outer, chunk, 2 * LANES), jnp.float32)],
            compiler_params=params(),
            name="azimuth_couple",
        )(lines, coupling, spatial, twist, fwd, inv, damp)

    def row_solve(field, edge):
        other, halo = neighbours(field, edge, n_depth * blocks)
        y, ends = pl.pallas_call(
            row_solve_kernel,
            out_shape=(f32(*grid_shape), f32(outer, 4 * terms, LANES)),
            in_specs=[smem(), smem()] + vmem(4),
            out_specs=tuple(vmem(2)),
            compiler_params=params(),
            name="row_solve",
        )(row_wave, core.astype(jnp.int32).reshape(1), field, other, halo, g_row)
        return pl.pallas_call(
            row_link_kernel,
            out_shape=f32(*grid_shape),
            in_specs=vmem(3),
            out_specs=vmem(1)[0],
            compiler_params=params(),
            name="row_link",
        )(y, sweeps(ends, all_columns, n_az), c_row)

    if by_block:
        ready = (damp, g_row, c_row, coupling, row_wave)
        advanced, ready = slab_solve(field, ready)
        damp, g_row, c_row, coupling, row_wave = ready
        lines = exchange(advanced, True)
        for step in range(STEPS):
            if step:
                lines = row_solve(lines, edge)
            lines, edge = couple(lines)
        field = exchange(lines, False)
    else:
        for _ in range(STEPS):
            advanced, damp = slab_solve(field, damp)
            lines = lax.all_to_all(advanced, "az", split_axis=0, concat_axis=0, tiled=True)
            coupled, _ = couple(lines)
            field = lax.all_to_all(coupled, "az", split_axis=0, concat_axis=0, tiled=True)
    return jnp.transpose(field, (1, 0, 2, 3)).reshape(parts, depth_rows, az_count)


def solution(mesh):
    in_specs = (
        P(None, "depth", "az"),
        P(None, None, "depth", None, None),
        P(None, None, "depth", None),
        P(None, None, "depth", None),
        P(),
        P(),
        P("depth"),
        P("depth"),
        P(),
        P("az"),
    )
    out_specs = P(None, "depth", "az")
    return jax.shard_map(local, mesh=mesh, in_specs=in_specs, out_specs=out_specs, check_vma=False)
```

```python
import functools
import math

import jax
import jax.numpy as jnp
import numpy as np
from jax import lax
from jax.experimental import pallas as pl
from jax.experimental.pallas import tpu as pltpu
from jax.sharding import PartitionSpec as P

STEPS = 2
LANES = 128
VMEM_BYTES = 48 * 1024 * 1024


def split(value):
    high = value.astype(jnp.bfloat16)
    low = (value - high.astype(jnp.float32)).astype(jnp.bfloat16)
    return high, low


def dot_split(left, right):
    def one(a, b):
        return jnp.dot(a, b, preferred_element_type=jnp.float32)

    return one(left[0], right[0]) + (one(left[0], right[1]) + one(left[1], right[0]))


def mul(a, b):
    return (a[0] * b[0] - a[1] * b[1], a[0] * b[1] + a[1] * b[0])


def sub(a, b):
    return (a[0] - b[0], a[1] - b[1])


def add(a, b):
    return (a[0] + b[0], a[1] + b[1])


def small_dft(values, sign):
    count = len(values)
    if count == 1:
        return values
    even = small_dft(values[0::2], sign)
    odd = small_dft(values[1::2], sign)
    half = count // 2
    low, high = [], []
    for k in range(half):
        re, im = odd[k]
        if k == 0:
            turned = (re, im)
        elif 4 * k == count:
            turned = (-sign * im, sign * re) if sign > 0 else (im, -re)
        elif 8 * k == count:
            root = math.sqrt(0.5)
            turned = ((re - sign * im) * root, (im + sign * re) * root)
        elif 8 * k == 3 * count:
            root = math.sqrt(0.5)
            turned = ((-re - sign * im) * root, (sign * re - im) * root)
        else:
            angle = 2.0 * math.pi * k / count
            turned = mul((re, im), (math.cos(angle), sign * math.sin(angle)))
        low.append(add(even[k], turned))
        high.append(sub(even[k], turned))
    return low + high


def cos_sin(x):
    turns = jnp.floor(x * (2.0 / math.pi) + 0.5)
    r = ((x - turns * 1.5703125) - turns * 4.837512969970703e-4) - turns * 7.549789948768648e-08
    q = turns.astype(jnp.int32)
    s = r * r
    sin_r = r + r * s * (-1.6666654611e-1 + s * (8.3321608736e-3 + s * -1.9515295891e-4))
    cos_r = (1.0 - 0.5 * s) + s * s * (
        4.166664568298827e-2 + s * (-1.388731625493765e-3 + s * 2.443315711809948e-5)
    )
    swap = (q & 1) == 1
    cos_x = jnp.where(swap, sin_r, cos_r)
    sin_x = jnp.where(swap, cos_r, sin_r)
    cos_x = jnp.where(((q + 1) & 2) == 2, -cos_x, cos_x)
    sin_x = jnp.where((q & 2) == 2, -sin_x, sin_x)
    return cos_x, sin_x


def parts8(rows):
    return (rows[0:8], rows[8:16])


def depth_kernel(wave_ref, p_ref, halo_ref, g_ref, col_ref, y_ref, ends_ref, sum_ref):
    blocks, block_rows = g_ref.shape[0], g_ref.shape[2] // 2
    chunk_rows = p_ref.shape[2]
    per = block_rows // chunk_rows
    lane_count = p_ref.shape[3]

    def block_of(part, b):
        return jnp.concatenate([p_ref[b * per + i, part] for i in range(per)], axis=0)

    firsts, lasts = [], []
    for b in range(blocks):
        own = [block_of(0, b), block_of(1, b)]
        lap = []
        for part in range(2):
            if b == 0:
                above = halo_ref[0, part : part + 1]
            else:
                above = p_ref[b * per - 1, part, chunk_rows - 1 : chunk_rows]
            if b == blocks - 1:
                below = halo_ref[1, part : part + 1]
            else:
                below = p_ref[(b + 1) * per, part, 0:1]
            up = jnp.concatenate([above, own[part][:-1]], axis=0)
            down = jnp.concatenate([own[part][1:], below], axis=0)
            lap.append(up + down - 2.0 * own[part])
        w_re, w_im = wave_ref[0, b], wave_ref[1, b]
        x = jnp.concatenate(
            [
                lap[0] + w_re * own[0] - w_im * own[1],
                lap[1] + w_re * own[1] + w_im * own[0],
            ],
            axis=0,
        )
        out = dot_split(split(g_ref[b]), split(x))
        for part in range(2):
            moved = own[part] + out[part * block_rows : (part + 1) * block_rows]
            for i in range(per):
                y_ref[b * per + i, part] = moved[i * chunk_rows : (i + 1) * chunk_rows]
        ends = out[2 * block_rows :]
        ends_ref[b] = ends
        firsts.append(parts8(ends[0:16]))
        lasts.append(parts8(ends[16:32]))
    zero = jnp.zeros((8, lane_count), jnp.float32)
    s = (zero, zero)
    heads = []
    for b in range(blocks):
        heads.append(sub(firsts[b], mul((col_ref[b, 2], col_ref[b, 3]), s)))
        s = sub(lasts[b], mul((col_ref[b, 0], col_ref[b, 1]), s))
    t = (zero, zero)
    for b in reversed(range(blocks)):
        t = sub(heads[b], mul((col_ref[b, 4], col_ref[b, 5]), t))
    sum_ref[...] = jnp.concatenate([s[0], s[1], t[0], t[1]], axis=0)


def link_kernel(here_ref, y_ref, ends_ref, sums_ref, col_ref, c_ref, out_ref):
    blocks = ends_ref.shape[0]
    devices = sums_ref.shape[0]
    chunk_rows = y_ref.shape[2]
    block_rows = c_ref.shape[1] // 2
    per = block_rows // chunk_rows
    here = here_ref[0]
    zero = jnp.zeros((8, y_ref.shape[3]), jnp.float32)

    def lam(b):
        return (col_ref[b, 0], col_ref[b, 1])

    def mu(b):
        return (col_ref[b, 2], col_ref[b, 3])

    def ups(b):
        return (col_ref[b, 4], col_ref[b, 5])

    entering = []
    s = (zero, zero)
    for d in range(devices):
        entering.append(s)
        if d < devices - 1:
            carried = s
            for b in range(d * blocks, (d + 1) * blocks):
                pair = mul(lam(b), carried)
                carried = (-pair[0], -pair[1])
            s = add(carried, parts8(sums_ref[d, 0:16]))
    leaving = [None] * devices
    t = (zero, zero)
    for d in reversed(range(devices)):
        leaving[d] = t
        if d > 0:
            carried = entering[d]
            heads = []
            for b in range(d * blocks, (d + 1) * blocks):
                pair = mul(mu(b), carried)
                heads.append((-pair[0], -pair[1]))
                pair = mul(lam(b), carried)
                carried = (-pair[0], -pair[1])
            back = t
            for b in reversed(range(d * blocks, (d + 1) * blocks)):
                back = sub(heads[b - d * blocks], mul(ups(b), back))
            t = add(back, parts8(sums_ref[d, 16:32]))
    s, t = entering[0], leaving[0]
    for d in range(1, devices):
        s = tuple(jnp.where(here == d, a, b) for a, b in zip(entering[d], s))
        t = tuple(jnp.where(here == d, a, b) for a, b in zip(leaving[d], t))

    def mine(b, k):
        return (col_ref[here * blocks + b, k], col_ref[here * blocks + b, k + 1])

    s_in, heads = [], []
    for b in range(blocks):
        s_in.append(s)
        first, last = parts8(ends_ref[b, 0:16]), parts8(ends_ref[b, 16:32])
        heads.append(sub(first, mul(mine(b, 2), s)))
        s = sub(last, mul(mine(b, 0), s))
    t_in = [None] * blocks
    for b in reversed(range(blocks)):
        t_in[b] = t
        t = sub(heads[b], mul(mine(b, 4), t))
    for b in range(blocks):
        carry = jnp.concatenate([s_in[b][0], s_in[b][1], t_in[b][0], t_in[b][1]], axis=0)
        fix = dot_split(split(c_ref[b]), split(carry))
        for part in range(2):
            for i in range(per):
                low = part * block_rows + i * chunk_rows
                out_ref[b * per + i, part] = y_ref[b * per + i, part] + fix[low : low + chunk_rows]


def azimuth_kernel(
    x_ref, c_ref, spatial_ref, twist_ref, fwd_ref, inv_ref, damp_ref, out_ref, edge_ref, held
):
    sources, rows, lane_count = x_ref.shape[0], x_ref.shape[2], x_ref.shape[3]
    tiles = lane_count // LANES
    outer = sources * tiles

    def where(a):
        return a // tiles, pl.ds((a % tiles) * LANES, LANES)

    @pl.loop(0, rows // 8)
    def _(g):
        at = pl.ds(pl.multiple_of(g * 8, 8), 8)
        values = []
        for a in range(outer):
            src, lanes = where(a)
            values.append((x_ref[src, 0, at, lanes], x_ref[src, 1, at, lanes]))
        for k, value in enumerate(small_dft(values, -1)):
            turned = mul(value, (twist_ref[0, k : k + 1], twist_ref[1, k : k + 1]))
            held[k, at, 0:LANES] = turned[0]
            held[k, at, LANES:] = turned[1]

    fwd = split(fwd_ref[...])
    inv = split(inv_ref[...])
    group = 4

    @pl.loop(0, outer // group)
    def _(g):
        at = pl.ds(g * group, group)
        x = held[at].reshape(group * rows, 2 * LANES)
        spec = dot_split(split(x), fwd).reshape(group, rows, 2 * LANES)
        turn_re, turn_im = cos_sin(c_ref[...][None] * spatial_ref[at])
        re, im = spec[..., :LANES], spec[..., LANES:]
        y = jnp.concatenate([re * turn_re + im * turn_im, im * turn_re - re * turn_im], axis=2)
        held[at] = dot_split(split(y.reshape(group * rows, 2 * LANES)), inv).reshape(
            group, rows, 2 * LANES
        )

    @pl.loop(0, rows // 8)
    def _(g):
        at = pl.ds(pl.multiple_of(g * 8, 8), 8)
        values = []
        for k in range(outer):
            value = (held[k, at, 0:LANES], held[k, at, LANES:])
            values.append(mul(value, (twist_ref[0, k : k + 1], -twist_ref[1, k : k + 1])))
        for a, value in enumerate(small_dft(values, 1)):
            src, lanes = where(a)
            damp = damp_ref[src, 0:1, lanes]
            out_ref[src, 0, at, lanes] = value[0] * damp
            out_ref[src, 1, at, lanes] = value[1] * damp

    for part in range(2):
        for src in range(sources):
            row = pl.ds(part * sources + src, 1)
            edge_ref[0, row] = out_ref[src, part, 0:1]
            edge_ref[1, row] = out_ref[src, part, rows - 1 : rows]


def tables(total):
    outer = total // LANES
    k1 = np.arange(outer)[:, None]
    a2 = np.arange(LANES)[None, :]
    angle = 2.0 * np.pi * ((k1 * a2) % total) / total
    twist = np.stack([np.cos(angle), -np.sin(angle)])
    angle = 2.0 * np.pi * ((np.arange(LANES)[:, None] * a2) % LANES) / LANES
    cos, sin = np.cos(angle), np.sin(angle)
    fwd = np.block([[cos, -sin], [sin, cos]])
    inv = np.block([[cos, sin], [-sin, cos]]) / total
    k = k1 + outer * a2
    signed = np.where(k < total // 2, k, k - total)
    spatial = ((2.0 * np.pi * signed / total) ** 2)[:, None, :]
    return [value.astype(np.float32) for value in (spatial, twist, fwd, inv)]


MESH_IDS = pl.DeviceIdType.MESH


def greet(devices):
    barrier = pltpu.get_barrier_semaphore()
    for present, device in devices:

        def tell(device=device):
            pl.semaphore_signal(barrier, inc=1, device_id=device, device_id_type=MESH_IDS)

        if present is None:
            tell()
        else:
            pl.when(present)(tell)
    amount = 0
    for present, _ in devices:
        amount = amount + (1 if present is None else jnp.where(present, 1, 0))
    pl.semaphore_wait(barrier, amount)


def remote(src, dst, send, recv, device):
    return pltpu.make_async_remote_copy(
        src_ref=src,
        dst_ref=dst,
        send_sem=send,
        recv_sem=recv,
        device_id=device,
        device_id_type=MESH_IDS,
    )


def exchange_kernel(forward, n, count, *refs):
    sources, targets = refs[:count], refs[count : 2 * count]
    send_sem, recv_sem = refs[2 * count :]
    depth, az = lax.axis_index("depth"), lax.axis_index("az")
    pair, core = depth // 2, depth % 2
    half = n // 2
    peers = []
    for step in range(1, 2 * n):
        other = (core * n + az + step) % (2 * n)
        peers.append((None, (2 * pair + other // n, other % n)))
    greet(peers)
    moves = []
    for step in range(n):
        j = (step + az) % n
        if forward:
            device = (2 * pair + j % 2, half * core + j // 2)
            slot = az
        else:
            device = (2 * pair + az // half, j)
            slot = 2 * (az % half) + core
        away = jnp.logical_or(device[0] != depth, device[1] != az)
        for i, (src_ref, dst_ref) in enumerate(zip(sources, targets)):
            arrive = recv_sem.at[i, slot]
            move = remote(src_ref.at[j], dst_ref.at[slot], send_sem.at[i, step], arrive, device)
            stay = pltpu.make_async_copy(src_ref.at[j], dst_ref.at[slot], arrive)
            pl.when(away)(move.start)
            pl.when(jnp.logical_not(away))(stay.start)
            moves.append((away, move))
    for slot in range(n):
        for i, (src_ref, dst_ref) in enumerate(zip(sources, targets)):
            pltpu.make_async_copy(src_ref.at[slot], dst_ref.at[slot], recv_sem.at[i, slot]).wait()
    for away, move in moves:
        pl.when(away)(move.wait_send)


def exchange(values, forward):
    n, count = values[0].shape[0], len(values)
    anywhere = [pl.BlockSpec(memory_space=pl.ANY)] * count
    return pl.pallas_call(
        functools.partial(exchange_kernel, forward, n, count),
        out_shape=tuple(jax.ShapeDtypeStruct(v.shape, v.dtype) for v in values),
        in_specs=anywhere,
        out_specs=tuple(anywhere),
        scratch_shapes=[pltpu.SemaphoreType.DMA((count, n))] * 2,
        compiler_params=pltpu.CompilerParams(
            collective_id=0 if forward else 1, has_side_effects=True
        ),
        name="exchange_out" if forward else "exchange_back",
    )(*values)


def neighbour_kernel(n, total_blocks, own_ref, edge_ref, other_ref, halo_ref, send_sem, recv_sem):
    depth, az = lax.axis_index("depth"), lax.axis_index("az")
    pair, core = depth // 2, depth % 2
    block = pair * n + az
    partner = (2 * pair + 1 - core, az)
    above, below = block > 0, block < total_blocks - 1

    def at(b, c):
        return (2 * (b // n) + c, b % n)

    greet(
        [(None, partner)]
        + [(above, at(block - 1, c)) for c in range(2)]
        + [(below, at(block + 1, c)) for c in range(2)]
    )
    sends = []
    for c in range(2):
        sends.append(
            (
                jnp.logical_and(below, core == 1),
                remote(
                    edge_ref.at[1], halo_ref.at[0], send_sem.at[1 + c], recv_sem.at[1], at(block + 1, c)
                ),
            )
        )
        sends.append(
            (
                jnp.logical_and(above, core == 0),
                remote(
                    edge_ref.at[0], halo_ref.at[1], send_sem.at[3 + c], recv_sem.at[2], at(block - 1, c)
                ),
            )
        )
    for present, move in sends:
        pl.when(present)(move.start)
    pieces = [
        remote(own_ref.at[i], other_ref.at[i], send_sem.at[5 + i], recv_sem.at[3 + i], partner)
        for i in range(n)
    ]
    for piece in pieces:
        piece.start()
    for side, present in ((0, above), (1, below)):
        got = pltpu.make_async_copy(edge_ref.at[side], halo_ref.at[side], recv_sem.at[1 + side])
        pl.when(present)(got.wait)

        @pl.when(jnp.logical_not(present))
        def _(side=side):
            halo_ref[side] = jnp.zeros(halo_ref.shape[1:], jnp.float32)

    for present, move in sends:
        pl.when(present)(move.wait_send)
    for piece in pieces:
        piece.wait()


def neighbours(field, edge, total_blocks):
    n = field.shape[0]
    return pl.pallas_call(
        functools.partial(neighbour_kernel, n, total_blocks),
        out_shape=(f32(*field.shape), f32(*edge.shape)),
        in_specs=[pl.BlockSpec(memory_space=pl.ANY), pl.BlockSpec(memory_space=pltpu.VMEM)],
        out_specs=(pl.BlockSpec(memory_space=pl.ANY), pl.BlockSpec(memory_space=pltpu.VMEM)),
        scratch_shapes=[pltpu.SemaphoreType.DMA((5 + n,)), pltpu.SemaphoreType.DMA((3 + n,))],
        compiler_params=pltpu.CompilerParams(collective_id=2, has_side_effects=True),
        name="neighbours",
    )(field, edge)


def row_solve_kernel(wave_ref, core_ref, own_ref, other_ref, halo_ref, g_ref, y_ref, ends_ref):
    sources, chunk_rows, lane_count = own_ref.shape[0], own_ref.shape[2], own_ref.shape[3]
    tiles = lane_count // LANES
    first = core_ref[0] == 0
    g = split(g_ref[...])
    w_re, w_im = wave_ref[0], wave_ref[1]
    for src in range(sources):
        own, lap, mine = [], [], []
        for part in range(2):
            here, there = own_ref[src, part], other_ref[src, part]
            top, bottom = jnp.where(first, here, there), jnp.where(first, there, here)
            row = part * sources + src
            rows = jnp.concatenate([top, bottom], axis=0)
            up = jnp.concatenate([halo_ref[0, row : row + 1], rows[:-1]], axis=0)
            down = jnp.concatenate([rows[1:], halo_ref[1, row : row + 1]], axis=0)
            own.append(rows)
            mine.append(here)
            lap.append(up + down - 2.0 * rows)
        x = jnp.concatenate(
            [
                lap[0] + w_re * own[0] - w_im * own[1],
                lap[1] + w_re * own[1] + w_im * own[0],
            ],
            axis=0,
        )
        out = dot_split(g, split(x))
        y_ref[src, 0] = mine[0] + out[:chunk_rows]
        y_ref[src, 1] = mine[1] + out[chunk_rows : 2 * chunk_rows]
        for tile in range(tiles):
            ends_ref[src * tiles + tile] = out[2 * chunk_rows :, tile * LANES : (tile + 1) * LANES]


def sweep_kernel(n, count, ends_ref, col_ref, out_ref, got, answer, sem_a, sem_b, sem_c, sem_d, sem_e):
    depth, az = lax.axis_index("depth"), lax.axis_index("az")
    pair, core = depth // 2, depth % 2
    block = pair * n + az
    partner = (2 * pair + 1 - core, az)

    def at(b):
        return (2 * (b // n) + core, b % n)

    others = [(block + step) % count for step in range(1, count)]
    greet([(None, partner)] + [(None, at(b)) for b in others])
    base = core * count
    moves = [
        remote(ends_ref.at[base + b], got.at[block], sem_a.at[i], sem_b.at[block], at(b))
        for i, b in enumerate(others)
    ]
    for move in moves:
        move.start()
    pltpu.make_async_copy(ends_ref.at[base + block], got.at[block], sem_b.at[block]).start()
    for b in range(count):
        pltpu.make_async_copy(ends_ref.at[b], got.at[b], sem_b.at[b]).wait()
    for move in moves:
        move.wait_send()
    zero = jnp.zeros((8, LANES), jnp.float32)
    s = (zero, zero)
    heads = []
    for b in range(count):
        first, last = parts8(got[b, 0:16]), parts8(got[b, 16:32])
        answer[b, 0:8] = s[0]
        answer[b, 8:16] = s[1]
        heads.append(sub(first, mul((col_ref[b, 2], col_ref[b, 3]), s)))
        s = sub(last, mul((col_ref[b, 0], col_ref[b, 1]), s))
    t = (zero, zero)
    for b in reversed(range(count)):
        answer[b, 16:24] = t[0]
        answer[b, 24:32] = t[1]
        t = sub(heads[b], mul((col_ref[b, 4], col_ref[b, 5]), t))
    moves = [
        remote(answer.at[b], out_ref.at[base + block], sem_a.at[i], sem_c.at[block], at(b))
        for i, b in enumerate(others)
    ]
    for move in moves:
        move.start()
    pltpu.make_async_copy(answer.at[block], out_ref.at[base + block], sem_c.at[block]).start()
    for b in range(count):
        pltpu.make_async_copy(answer.at[b], out_ref.at[base + b], sem_c.at[b]).wait()
    for move in moves:
        move.wait_send()
    rows = out_ref.at[pl.ds(base, count)]
    swap = remote(rows, rows, sem_d.at[0], sem_e.at[0], partner)
    swap.start()
    swap.wait()


def sweeps(ends, columns, n):
    count = columns.shape[0]
    dma = pltpu.SemaphoreType.DMA
    return pl.pallas_call(
        functools.partial(sweep_kernel, n, count),
        out_shape=f32(*ends.shape),
        in_specs=vmem(2),
        out_specs=vmem(1)[0],
        scratch_shapes=[
            pltpu.VMEM((count, 32, LANES), jnp.float32),
            pltpu.VMEM((count, 32, LANES), jnp.float32),
            dma((count - 1,)),
            dma((count,)),
            dma((count,)),
            dma((1,)),
            dma((1,)),
        ],
        compiler_params=pltpu.CompilerParams(collective_id=3, has_side_effects=True),
        name="sweeps",
    )(ends, columns)


def row_link_kernel(y_ref, carry_ref, c_ref, out_ref):
    sources, chunk_rows, lane_count = y_ref.shape[0], y_ref.shape[2], y_ref.shape[3]
    tiles = lane_count // LANES
    c = split(c_ref[...])
    for src in range(sources):
        carry = jnp.concatenate([carry_ref[src * tiles + i] for i in range(tiles)], axis=1)
        fix = dot_split(c, split(carry))
        for part in range(2):
            out_ref[src, part] = y_ref[src, part] + fix[part * chunk_rows : (part + 1) * chunk_rows]


def vmem(count):
    return [pl.BlockSpec(memory_space=pltpu.VMEM)] * count


def smem():
    return pl.BlockSpec(memory_space=pltpu.SMEM)


def params():
    return pltpu.CompilerParams(vmem_limit_bytes=VMEM_BYTES)


def f32(*shape):
    return jax.ShapeDtypeStruct(shape, jnp.float32)


def weighted(inverses, lower, upper, weights):
    w_re, w_im = weights[0], weights[1]

    def total(re, im):
        shape = (-1,) + (1,) * (re.ndim - 1)
        a, b = w_re.reshape(shape), w_im.reshape(shape)
        return a * re - b * im, a * im + b * re

    m_re, m_im = total(inverses[0], inverses[1])
    m_re, m_im = m_re.sum(0), m_im.sum(0)

    def real_rows(re, im):
        return [jnp.concatenate([re, -im], axis=-1), jnp.concatenate([im, re], axis=-1)]

    first = jnp.moveaxis(inverses[:, :, :, 0], 1, 2)
    last = jnp.moveaxis(inverses[:, :, :, -1], 1, 2)
    g = jnp.concatenate(
        real_rows(m_re, m_im) + real_rows(first[0], first[1]) + real_rows(last[0], last[1]), axis=1
    )
    wl_re, wl_im = (jnp.transpose(v, (1, 2, 0)) for v in total(lower[0], lower[1]))
    wu_re, wu_im = (jnp.transpose(v, (1, 2, 0)) for v in total(upper[0], upper[1]))
    c = jnp.concatenate(
        [
            jnp.concatenate([-wl_re, wl_im, -wu_re, wu_im], axis=-1),
            jnp.concatenate([-wl_im, -wl_re, -wu_im, -wu_re], axis=-1),
        ],
        axis=1,
    )
    return g, c


def local(
    pressure_field,
    block_inverses,
    lower_spikes,
    upper_spikes,
    pade_weights,
    layer_wavenumber,
    layer_index,
    depth_coupling,
    attenuation,
    sediment_type,
):
    parts, depth_rows, az_count = pressure_field.shape
    blocks, block_rows = block_inverses.shape[2], block_inverses.shape[3]
    n_az, n_depth = lax.axis_size("az"), lax.axis_size("depth")
    chunk = depth_rows // n_az
    total = n_az * az_count
    outer = total // LANES
    az_at = lax.axis_index("az")
    spatial, twist, fwd, inv = (jnp.asarray(v) for v in tables(total))
    g, c = weighted(block_inverses, lower_spikes, upper_spikes, pade_weights)
    terms = pade_weights.shape[1]
    columns = jnp.stack(
        [
            lower_spikes[0, :, :, -1],
            lower_spikes[1, :, :, -1],
            lower_spikes[0, :, :, 0],
            lower_spikes[1, :, :, 0],
            upper_spikes[0, :, :, 0],
            upper_spikes[1, :, :, 0],
        ]
    )
    columns = jnp.transpose(columns, (2, 0, 1))
    all_columns = lax.all_gather(columns, "depth").reshape(n_depth * blocks, 6, terms, 1)
    columns = columns.reshape(blocks, 6, terms, 1)
    wave = layer_wavenumber[:, layer_index]
    depth_at = lax.axis_index("depth")
    by_block = (
        n_az == 2 * blocks
        and n_depth % 2 == 0
        and 2 * chunk == block_rows
        and n_depth * n_az * LANES == total
    )
    if by_block:
        core = depth_at % 2
        picked = (
            lax.dynamic_index_in_dim(g, az_at % blocks, keepdims=False),
            lax.dynamic_index_in_dim(c, az_at % blocks, keepdims=False),
            lax.dynamic_slice_in_dim(layer_index, az_at % blocks, 1),
            lax.dynamic_slice_in_dim(depth_coupling, az_at % blocks * block_rows, block_rows),
        )
        swap = [(i, i + 1 - 2 * (i % 2)) for i in range(n_depth)]
        other = jax.tree.map(lambda v: lax.ppermute(v, "depth", swap), picked)
        mine = core == az_at // blocks
        g_row, c_row, layer, coupling = jax.tree.map(
            lambda a, b: jnp.where(mine, a, b), picked, other
        )
        layer = layer[0]

        def half(value, start):
            return lax.dynamic_slice_in_dim(value, start + core * chunk, chunk)

        g_row = jnp.concatenate([half(g_row, 0), half(g_row, block_rows), g_row[2 * block_rows :]])
        c_row = jnp.concatenate([half(c_row, 0), half(c_row, block_rows)])
        coupling = half(coupling, 0).reshape(chunk, 1)
        row_wave = lax.dynamic_index_in_dim(layer_wavenumber, layer, axis=1, keepdims=False)
    else:
        layer = lax.dynamic_index_in_dim(layer_index, az_at * chunk // block_rows, keepdims=False)
        coupling = lax.dynamic_slice_in_dim(depth_coupling, az_at * chunk, chunk).reshape(chunk, 1)
    if by_block:
        types, fade = sediment_type[None], attenuation[layer_index]
    else:
        types = lax.all_gather(sediment_type, "az")
        fade = lax.dynamic_slice_in_dim(attenuation, layer, 1)
    exponent = jnp.zeros(jnp.broadcast_shapes(types.shape, (fade.shape[0], 1)), jnp.float32)
    for kind in range(attenuation.shape[1]):
        exponent = jnp.where(types == kind, fade[:, kind : kind + 1], exponent)
    damp = jnp.exp(-exponent)
    damp = jnp.repeat(damp, n_az // damp.shape[0], axis=0)[:, None]
    here = lax.axis_index("depth").astype(jnp.int32).reshape(1)
    grid_shape = (n_az, parts, chunk, az_count)
    field = jnp.transpose(pressure_field.reshape(parts, n_az, chunk, az_count), (1, 0, 2, 3))
    down = [(i, i + 1) for i in range(n_depth - 1)]
    up = [(i + 1, i) for i in range(n_depth - 1)]

    def slab_solve(field, ready):
        halo = jnp.stack(
            [
                lax.ppermute(field[-1, :, -1], "depth", down),
                lax.ppermute(field[0, :, 0], "depth", up),
            ]
        )
        y, ends, sums = pl.pallas_call(
            depth_kernel,
            out_shape=(
                f32(*grid_shape),
                f32(blocks, 4 * terms, az_count),
                f32(4 * terms, az_count),
            ),
            in_specs=[smem()] + vmem(4),
            out_specs=tuple(vmem(3)),
            compiler_params=params(),
            name="depth_solve",
        )(wave, field, halo, g, columns)
        all_sums = lax.all_gather(sums, "depth")
        y, ready = lax.optimization_barrier((y, ready))
        advanced = pl.pallas_call(
            link_kernel,
            out_shape=f32(*grid_shape),
            in_specs=[smem()] + vmem(5),
            out_specs=vmem(1)[0],
            compiler_params=params(),
            name="depth_link",
        )(here, y, ends, all_sums, all_columns, c)
        return advanced, ready

    def couple(lines):
        return pl.pallas_call(
            azimuth_kernel,
            out_shape=(f32(*grid_shape), f32(2, parts * n_az, az_count)),
            in_specs=vmem(7),
            out_specs=tuple(vmem(2)),
            scratch_shapes=[pltpu.VMEM((outer, chunk, 2 * LANES), jnp.float32)],
            compiler_params=params(),
            name="azimuth_couple",
        )(lines, coupling, spatial, twist, fwd, inv, damp)

    def row_solve(field, edge):
        other, halo = neighbours(field, edge, n_depth * blocks)
        y, ends = pl.pallas_call(
            row_solve_kernel,
            out_shape=(f32(*grid_shape), f32(outer, 4 * terms, LANES)),
            in_specs=[smem(), smem()] + vmem(4),
            out_specs=tuple(vmem(2)),
            compiler_params=params(),
            name="row_solve",
        )(row_wave, core.astype(jnp.int32).reshape(1), field, other, halo, g_row)
        return pl.pallas_call(
            row_link_kernel,
            out_shape=f32(*grid_shape),
            in_specs=vmem(3),
            out_specs=vmem(1)[0],
            compiler_params=params(),
            name="row_link",
        )(y, sweeps(ends, all_columns, n_az), c_row)

    if by_block:
        ready = (damp, g_row, c_row, coupling, row_wave)
        advanced, ready = slab_solve(field, ready)
        damp, g_row, c_row, coupling, row_wave = ready
        lines, damp = exchange((advanced, damp), True)
        for step in range(STEPS):
            if step:
                lines = row_solve(lines, edge)
            lines, edge = couple(lines)
        (field,) = exchange((lines,), False)
    else:
        for _ in range(STEPS):
            advanced, damp = slab_solve(field, damp)
            lines = lax.all_to_all(advanced, "az", split_axis=0, concat_axis=0, tiled=True)
            coupled, _ = couple(lines)
            field = lax.all_to_all(coupled, "az", split_axis=0, concat_axis=0, tiled=True)
    return jnp.transpose(field, (1, 0, 2, 3)).reshape(parts, depth_rows, az_count)


def solution(mesh):
    in_specs = (
        P(None, "depth", "az"),
        P(None, None, "depth", None, None),
        P(None, None, "depth", None),
        P(None, None, "depth", None),
        P(),
        P(),
        P("depth"),
        P("depth"),
        P(),
        P("az"),
    )
    out_specs = P(None, "depth", "az")
    return jax.shard_map(local, mesh=mesh, in_specs=in_specs, out_specs=out_specs, check_vma=False)
```
